256 devices in a mesh: dp: 32 (over x, z), tensor: 8 (over y, core).
Axes of the slice: x: 4, y: 4, z: 8, core: 2. Of those that a mesh axis runs over, the one named last changes fastest.
Arguments:
- activations: bfloat16 [28672, 1024], P('dp'), may hold values from -6 to 6
- output_grads: bfloat16 [28672, 14784], P('dp', 'tensor'), may hold values from -0.1875 to 0.1875
- error_buffer: bfloat16 [32, 1024, 14784], P('dp', None, 'tensor'), may hold values from -4 to 4
- right_start: bfloat16 [14784, 64], P('tensor'), may hold values from -0.046875 to 0.046875
Outputs:
- left_factor: float32 [1024, 64], replicated
- right_factor: bfloat16 [14784, 64], P('tensor')
- new_error: bfloat16 [32, 1024, 14784], P('dp', None, 'tensor')
The draws below stay inside these ranges and needn't reach their ends.
All inputs are finite; a program needn't handle non-finite values.
Results may differ from the reference program's by a relative error of at most 0.0062.
Values sent between devices are 32-bit elements; how exact they have to be, the bound alone decides.
No kernel may reach another device: no remote copies, remote signals or barrier semaphores. Data moves between devices by JAX's collectives and lax.ppermute only.
A program may use at most 64 MiB of HBM per device.

```python
import jax
import jax.numpy as jnp
from jax import lax

ROWS = 1024
COLS = 14784
RANK = 64
TOK = 896
N_DP = 32


def block_scale(own_key, extent, cuts, least, high):
    loudness = 1.0
    for position, shards_of in cuts:
        heights = jax.random.uniform(jax.random.fold_in(jax.random.fold_in(own_key, 6), position), (shards_of,), jnp.float32, least / len(cuts), high / len(cuts))
        loudness = loudness * jnp.repeat(jnp.exp(heights), extent[position] // shards_of).reshape((-1,) + (1,) * (len(extent) - 1 - position))
    return loudness


def scatter_about(rng, shape, width, bound, shards=(), kind=jnp.bfloat16):
    result = jax.random.normal(rng, shape, jnp.float32) * width
    if len(shards) > 0:
        result = block_scale(rng, shape, shards, -0.22, 0.18) * result
    return jnp.clip(result, min=-bound, max=bound).astype(kind)


def setup_inputs(seed: int = 0) -> dict:
    keys = jax.random.split(jax.random.key(seed), 5)
    activations = scatter_about(keys[0], (N_DP * TOK, ROWS), 1.0, 6.0, ((0, 32),))
    output_grads = scatter_about(keys[1], (N_DP * TOK, COLS), TOK ** -0.5, 0.1875, ((0, 32), (1, 8)))
    error_buffer = scatter_about(keys[2], (N_DP, ROWS, COLS), 0.5, 4.0, ((0, 32), (2, 8)))
    right_start = scatter_about(keys[3], (COLS, RANK), COLS ** -0.5, 0.046875, ((0, 8),))
    return dict(activations=activations, output_grads=output_grads, error_buffer=error_buffer, right_start=right_start)


def reference(activations, output_grads, error_buffer, right_start):

    def accumulate(replica):
        inputs = lax.dynamic_slice_in_dim(activations, replica * TOK, TOK, 0)
        upstream = lax.dynamic_slice_in_dim(output_grads, replica * TOK, TOK, 0)
        gradient = lax.dot_general(inputs.astype(jnp.float32), upstream.astype(jnp.float32), (((0,), (0,)), ((), ())), preferred_element_type=jnp.float32)
        own_error = lax.dynamic_index_in_dim(error_buffer, replica, 0, keepdims=False)
        return (own_error.astype(jnp.float32) + gradient).astype(jnp.bfloat16)
    accumulated = lax.map(accumulate, jnp.arange(N_DP, dtype=jnp.int32))

    def left_step(carry, block_acc):
        return (carry + jnp.dot(block_acc.astype(jnp.float32), right_start.astype(jnp.float32), preferred_element_type=jnp.float32), None)
    left_sum, unused = lax.scan(left_step, jnp.zeros((ROWS, RANK), jnp.float32), accumulated)
    left_mean = left_sum / N_DP
    gram = lax.dot_general(left_mean, left_mean, (((0,), (0,)), ((), ())), precision=lax.Precision.HIGHEST)
    lower = jnp.linalg.cholesky(gram)
    left_factor = jax.scipy.linalg.solve_triangular(lower, left_mean.T, lower=True).T
    left_low = left_factor.astype(jnp.bfloat16)

    def right_step(carry, block_acc):
        term = lax.dot_general(block_acc.astype(jnp.float32), left_low.astype(jnp.float32), (((0,), (0,)), ((), ())), preferred_element_type=jnp.float32)
        return (carry + term, None)
    right_sum, unused = lax.scan(right_step, jnp.zeros((COLS, RANK), jnp.float32), accumulated)
    right_factor = (right_sum / N_DP).astype(jnp.bfloat16)
    update = lax.dot_general(left_low.astype(jnp.float32), right_factor.astype(jnp.float32), (((1,), (1,)), ((), ())), preferred_element_type=jnp.float32)

    def residue(block_acc):
        return (block_acc.astype(jnp.float32) - update).astype(jnp.bfloat16)
    new_error = lax.map(residue, accumulated)
    return (left_factor, right_factor, new_error)
```

```python
import jax
import jax.numpy as jnp
from jax import lax
from jax.sharding import PartitionSpec as P

ALL = ("dp", "tensor")


def gram_of(matrix):
    return lax.dot_general(
        matrix, matrix, (((0,), (0,)), ((), ())), precision=lax.Precision.HIGHEST
    )


def orthonormal(matrix, lower):
    return jax.scipy.linalg.solve_triangular(lower, matrix.T, lower=True).T


def sum_over(pieces, axes):
    count = pieces.shape[0]
    arrived = lax.all_to_all(pieces, axes, 0, 0, tiled=True)
    total = jnp.sum(arrived, axis=0, keepdims=True)
    return lax.all_to_all(
        jnp.broadcast_to(total, pieces.shape), axes, 0, 0, tiled=True
    )


def local(activations, output_grads, error_buffer, right_start):
    gradient = lax.dot_general(
        activations, output_grads, (((0,), (0,)), ((), ())), preferred_element_type=jnp.float32
    )
    accumulated = (error_buffer[0].astype(jnp.float32) + gradient).astype(jnp.bfloat16)
    replicas = lax.axis_size("dp")
    devices = replicas * lax.axis_size("tensor")
    rows, rank = accumulated.shape[0], right_start.shape[1]
    partial_value = lax.dot_general(
        right_start, accumulated, (((0,), (1,)), ((), ())), preferred_element_type=jnp.float32
    )
    blocks = rows // 128
    pieces = partial_value.reshape(rank, blocks, 128).transpose(1, 0, 2)
    pieces = pieces.reshape(devices, rank * blocks // devices, 128)
    summed = sum_over(pieces, ALL).reshape(blocks, rank, 128)
    summed = summed.transpose(0, 2, 1).reshape(rows, rank)
    left_mean = summed / replicas
    lower = jnp.linalg.cholesky(gram_of(left_mean))
    left_factor = orthonormal(left_mean, lower)
    left_low = left_factor.astype(jnp.bfloat16)
    right_part = lax.dot_general(
        left_low, accumulated, (((0,), (0,)), ((), ())), preferred_element_type=jnp.float32
    )
    columns = right_part.shape[1]
    pieces = right_part.reshape(replicas, rank // replicas, columns)
    right_sum = sum_over(pieces, "dp").reshape(rank, columns)
    right_factor = (right_sum / replicas).astype(jnp.bfloat16).T
    update = lax.dot_general(
        left_low, right_factor, (((1,), (1,)), ((), ())), preferred_element_type=jnp.float32
    )
    new_error = (accumulated.astype(jnp.float32) - update).astype(jnp.bfloat16)
    return (left_factor, right_factor, new_error[None])


def solution(mesh):
    return jax.shard_map(
        local,
        mesh=mesh,
        in_specs=(P("dp", None), P("dp", "tensor"), P("dp", None, "tensor"), P("tensor", None)),
        out_specs=(P(), P("tensor", None), P("dp", None, "tensor")),
        check_vma=False,
    )
```

```python
import functools

import jax
import jax.numpy as jnp
from jax import lax
from jax.experimental import pallas as pl
from jax.experimental.pallas import tpu as pltpu
from jax.sharding import Mesh, PartitionSpec as P

ROWS, COLS, RANK, TOK, N_DP = 1024, 1848, 64, 896, 32
LANES = 128
ROW_TILES = ROWS // LANES
COL_TILES = -(-COLS // LANES)
HALF = 1024
HALVES = (HALF, COLS - HALF)
CHUNKS = ((0, 0, 512), (0, 512, 512), (1, 0, 512), (1, 512, COLS - HALF - 512))
DP = ("x", "z")
PLANE = ("x", "y", "core")
VMEM_LIMIT = 53 * 2**20
LEFT_LIMIT = 56 * 2**20
HIGHEST = lax.Precision.HIGHEST
ANY = pl.BlockSpec(memory_space=pl.ANY)
WHOLE = pl.BlockSpec(memory_space=pltpu.VMEM)


def params(limit=VMEM_LIMIT):
    return pltpu.CompilerParams(vmem_limit_bytes=limit)


def split(value):
    high = value.astype(jnp.bfloat16)
    rest = value - high.astype(jnp.float32)
    middle = rest.astype(jnp.bfloat16)
    low = (rest - middle.astype(jnp.float32)).astype(jnp.bfloat16)
    return high, middle, low


def add_parts(product):
    return product[:RANK] + (product[RANK : 2 * RANK] + product[2 * RANK :])


def whole_copies(sources, targets, sems):
    return [
        pltpu.make_async_copy(source, target, sems.at[i])
        for i, (source, target) in enumerate(zip(sources, targets))
    ]


def left_kernel(
    act_hbm, grad_hbm, error_hbm, right_hbm, left_ref,
    act_ref, grad_ref, error_ref, right_ref, sems,
):
    act_copy, grad_copy, error_copy, right_copy = whole_copies(
        (act_hbm, grad_hbm, error_hbm, right_hbm),
        (act_ref, grad_ref, error_ref, right_ref),
        sems,
    )
    right_copy.start()
    grad_copy.start()
    act_copy.start()
    error_copy.start()
    right_copy.wait()
    grad_copy.wait()
    inner = jnp.dot(right_ref[...], grad_ref[...], preferred_element_type=jnp.float32)
    parts = jnp.concatenate(split(inner), axis=0)
    act_copy.wait()
    total = add_parts(jnp.dot(parts, act_ref[...], preferred_element_type=jnp.float32))
    error_copy.wait()
    total = total + jnp.dot(right_ref[...], error_ref[...], preferred_element_type=jnp.float32)
    for tile in range(ROW_TILES):
        left_ref[pl.ds(tile * RANK, RANK), :] = total[:, tile * LANES : (tile + 1) * LANES]


def left_term(act, grad, error, right):
    return pl.pallas_call(
        left_kernel,
        in_specs=[ANY] * 4,
        out_specs=WHOLE,
        out_shape=jax.ShapeDtypeStruct((ROW_TILES * RANK, LANES), jnp.float32),
        scratch_shapes=[
            pltpu.VMEM((TOK, ROWS), jnp.bfloat16),
            pltpu.VMEM((COLS, TOK), jnp.bfloat16),
            pltpu.VMEM((COLS, ROWS), jnp.bfloat16),
            pltpu.VMEM((RANK, COLS), jnp.bfloat16),
            pltpu.SemaphoreType.DMA((4,)),
        ],
        compiler_params=params(LEFT_LIMIT),
        cost_estimate=pl.CostEstimate(
            flops=2 * RANK * (COLS * (ROWS + TOK) + ROWS * TOK),
            bytes_accessed=9_000_000, transcendentals=0,
        ),
        name="left_term",
    )(act, grad, error, right)


def accumulate_kernel(
    half, act_hbm, grad_hbm, error_hbm, acc_hbm,
    act_ref, grad_ref, error_ref, acc_ref, sems, grad_sems, error_sems, acc_sems,
):
    chunks = [(i, a, n) for i, (h, a, n) in enumerate(c for c in CHUNKS if c[0] == half)]
    act_copy = pltpu.make_async_copy(act_hbm, act_ref, sems.at[0])
    grad_copies, error_copies, acc_copies = [], [], []
    act_copy.start()
    for i, a, n in chunks:
        here, there = pl.ds(a, n), pl.ds(half * HALF + a, n)
        grad_copies.append(
            pltpu.make_async_copy(grad_hbm.at[there], grad_ref.at[here], grad_sems.at[i])
        )
        error_copies.append(
            pltpu.make_async_copy(error_hbm.at[there], error_ref.at[here], error_sems.at[i])
        )
        acc_copies.append(
            pltpu.make_async_copy(acc_ref.at[here], acc_hbm.at[here], acc_sems.at[i])
        )
        grad_copies[i].start()
        error_copies[i].start()
    act_copy.wait()
    for i, a, n in chunks:
        rows = pl.ds(a, n)
        grad_copies[i].wait()
        gradient = jnp.dot(grad_ref[rows, :], act_ref[...], preferred_element_type=jnp.float32)
        error_copies[i].wait()
        acc_ref[rows, :] = (error_ref[rows, :].astype(jnp.float32) + gradient).astype(jnp.bfloat16)
        acc_copies[i].start()
    for copy in acc_copies:
        copy.wait()


def accumulate(half, act, grad, error):
    size = HALVES[half]
    return pl.pallas_call(
        functools.partial(accumulate_kernel, half),
        in_specs=[ANY] * 3,
        out_specs=ANY,
        out_shape=jax.ShapeDtypeStruct((size, ROWS), jnp.bfloat16),
        scratch_shapes=[
            pltpu.VMEM((TOK, ROWS), jnp.bfloat16),
            pltpu.VMEM((size, TOK), jnp.bfloat16),
            pltpu.VMEM((size, ROWS), jnp.bfloat16),
            pltpu.VMEM((size, ROWS), jnp.bfloat16),
            pltpu.SemaphoreType.DMA((1,)),
            pltpu.SemaphoreType.DMA((2,)),
            pltpu.SemaphoreType.DMA((2,)),
            pltpu.SemaphoreType.DMA((2,)),
        ],
        compiler_params=params(56 * 2**20),
        cost_estimate=pl.CostEstimate(
            flops=2 * size * ROWS * TOK, bytes_accessed=8_000_000, transcendentals=0
        ),
        name="accumulate",
    )(act, grad, error)


def chunk_copies(sources, targets, sems):
    return [
        pltpu.make_async_copy(
            sources[h].at[pl.ds(a, n)], targets[h].at[pl.ds(a, n)], sems.at[i]
        )
        for i, (h, a, n) in enumerate(CHUNKS)
    ]


def project_kernel(left_ref, acc_a, acc_b, out_ref, parts_ref, half_a, half_b, sems):
    acc = (half_a, half_b)
    copies = chunk_copies((acc_a, acc_b), acc, sems)
    for copy in copies:
        copy.start()
    for tile in range(ROW_TILES):
        lanes = pl.ds(tile * LANES, LANES)
        mean = left_ref[pl.ds(tile * RANK, RANK), :] * (1.0 / N_DP)
        for i, part in enumerate(split(mean)):
            parts_ref[pl.ds(i * RANK, RANK), lanes] = part
    parts = parts_ref[...]
    for i, (h, a, n) in enumerate(CHUNKS):
        copies[i].wait()
        product = lax.dot_general(
            parts, acc[h][pl.ds(a, n), :], (((1,), (1,)), ((), ())),
            preferred_element_type=jnp.float32,
        )
        total = add_parts(product)
        for tile in range(-(-n // LANES)):
            piece = total[:, tile * LANES : min(n, (tile + 1) * LANES)]
            spare = LANES - piece.shape[1]
            if spare:
                piece = jnp.concatenate([piece, jnp.zeros((RANK, spare), jnp.float32)], axis=1)
            out_ref[pl.ds(((h * HALF + a) // LANES + tile) * RANK, RANK), :] = piece


def project(left_sum, acc_a, acc_b):
    return pl.pallas_call(
        project_kernel,
        in_specs=[WHOLE, ANY, ANY],
        out_specs=WHOLE,
        out_shape=jax.ShapeDtypeStruct((COL_TILES * RANK, LANES), jnp.float32),
        scratch_shapes=[
            pltpu.VMEM((3 * RANK, ROWS), jnp.bfloat16),
            pltpu.VMEM((HALVES[0], ROWS), jnp.bfloat16),
            pltpu.VMEM((HALVES[1], ROWS), jnp.bfloat16),
            pltpu.SemaphoreType.DMA((len(CHUNKS),)),
        ],
        compiler_params=params(),
        cost_estimate=pl.CostEstimate(
            flops=6 * COLS * ROWS * RANK, bytes_accessed=4_500_000, transcendentals=0
        ),
        name="project",
    )(left_sum, acc_a, acc_b)


def finish_kernel(
    sum_ref, inverse_ref, left_ref, acc_a, acc_b, right_hbm, error_hbm,
    half_a, half_b, right_ref, error_ref, sems, right_sem, error_sems,
):
    acc = (half_a, half_b)
    copies = chunk_copies((acc_a, acc_b), acc, sems)
    starts = [h * HALF + a for h, a, n in CHUNKS]
    error_copies = [
        pltpu.make_async_copy(
            error_ref.at[pl.ds(start, chunk[2])],
            error_hbm.at[pl.ds(start, chunk[2])],
            error_sems.at[i],
        )
        for i, (start, chunk) in enumerate(zip(starts, CHUNKS))
    ]
    right_copy = pltpu.make_async_copy(right_ref, right_hbm, right_sem.at[0])
    for copy in copies:
        copy.start()
    terms = jnp.concatenate(
        [sum_ref[pl.ds(tile * RANK, RANK), :] for tile in range(COL_TILES)], axis=1
    )
    right = jnp.dot(
        inverse_ref[...], terms, precision=HIGHEST, preferred_element_type=jnp.float32
    )
    right = (right * (1.0 / N_DP)).astype(jnp.bfloat16)
    right_ref[...] = right[:, :COLS]
    right_copy.start()
    left = left_ref[...]
    for i, (h, a, n) in enumerate(CHUNKS):
        start = starts[i]
        update = lax.dot_general(
            right_ref[:, start : start + n], left, (((0,), (0,)), ((), ())),
            preferred_element_type=jnp.float32,
        )
        copies[i].wait()
        held = acc[h][pl.ds(a, n), :].astype(jnp.float32)
        error_ref[pl.ds(start, n), :] = (held - update).astype(jnp.bfloat16)
        error_copies[i].start()
    right_copy.wait()
    for copy in error_copies:
        copy.wait()


def finish(right_sum, inverse, left_low, acc_a, acc_b):
    return pl.pallas_call(
        finish_kernel,
        in_specs=[WHOLE, WHOLE, WHOLE, ANY, ANY],
        out_specs=[ANY, ANY],
        out_shape=[
            jax.ShapeDtypeStruct((RANK, COLS), jnp.bfloat16),
            jax.ShapeDtypeStruct((COLS, ROWS), jnp.bfloat16),
        ],
        scratch_shapes=[
            pltpu.VMEM((HALVES[0], ROWS), jnp.bfloat16),
            pltpu.VMEM((HALVES[1], ROWS), jnp.bfloat16),
            pltpu.VMEM((RANK, COLS), jnp.bfloat16),
            pltpu.VMEM((COLS, ROWS), jnp.bfloat16),
            pltpu.SemaphoreType.DMA((len(CHUNKS),)),
            pltpu.SemaphoreType.DMA((1,)),
            pltpu.SemaphoreType.DMA((len(CHUNKS),)),
        ],
        compiler_params=params(),
        cost_estimate=pl.CostEstimate(
            flops=2 * COLS * ROWS * RANK, bytes_accessed=8_500_000, transcendentals=0
        ),
        name="finish",
    )(right_sum, inverse, left_low, acc_a, acc_b)


def exchange(pieces, axes):
    return lax.all_to_all(pieces, axes, 0, 0, tiled=True)


def spread(total, count):
    return jnp.broadcast_to(total[None], (count,) + total.shape)


def sum_left(part, work):
    mine = jnp.sum(exchange(part.reshape(32, 16, LANES), PLANE), axis=0)
    mine, first = lax.optimization_barrier((mine, work[0]))
    mine = jnp.sum(exchange(spread(mine, 8), "z"), axis=0)
    mine, second = lax.optimization_barrier((mine, work[1]))
    return exchange(spread(mine, 32), PLANE).reshape(part.shape), (first, second)


def sum_right(part):
    mine = jnp.sum(exchange(part.reshape(32, 15, 2, LANES), DP), axis=0)
    return exchange(spread(mine, 32), DP).reshape(part.shape)


def orthonormal(left_sum):
    mean = left_sum.reshape(ROW_TILES, RANK, LANES).transpose(1, 0, 2).reshape(RANK, ROWS)
    mean = mean / N_DP
    gram = lax.dot_general(mean, mean, (((1,), (1,)), ((), ())), precision=HIGHEST)
    lower = jnp.linalg.cholesky(gram)
    inverse = jax.scipy.linalg.solve_triangular(lower, jnp.eye(RANK, dtype=jnp.float32), lower=True)
    return inverse, jnp.dot(inverse, mean, precision=HIGHEST)


def local(activations, output_grads, error_buffer, right_start):
    grad, error = output_grads.T, error_buffer[0].T
    left_part = left_term(activations, grad, error, right_start.T)
    acc = [accumulate(half, activations, grad, error) for half in range(2)]
    left_sum, acc = sum_left(left_part, acc)
    right_sum = sum_right(project(left_sum, *acc))
    inverse, left = orthonormal(left_sum)
    right, new_error = finish(right_sum, inverse, left.astype(jnp.bfloat16), *acc)
    return (left.T, right.T, new_error.T[None])


def solution(mesh):
    fine = Mesh(mesh.devices.reshape(4, 8, 4, 2), ("x", "z", "y", "core"))
    tensor = ("y", "core")
    return jax.shard_map(
        local,
        mesh=fine,
        in_specs=(P(DP, None), P(DP, tensor), P(DP, None, tensor), P(tensor, None)),
        out_specs=(P(), P(tensor, None), P(DP, None, tensor)),
        check_vma=False,
    )
```

```python
import functools

import jax
import jax.numpy as jnp
from jax import lax
from jax.experimental import pallas as pl
from jax.experimental.pallas import tpu as pltpu
from jax.sharding import Mesh, PartitionSpec as P

ROWS, COLS, RANK, TOK, N_DP = 1024, 1848, 64, 896, 32
LANES = 128
ROW_TILES = ROWS // LANES
COL_TILES = -(-COLS // LANES)
HALF = 1024
HALVES = (HALF, COLS - HALF)
CHUNKS = ((0, 0, 512), (0, 512, 512), (1, 0, 512), (1, 512, COLS - HALF - 512))
Z = ("zh", "zl")
DP = ("x",) + Z
NEAR = ("x", "zl")
PLANE = ("x", "y", "core")
VMEM_LIMIT = 53 * 2**20
LEFT_LIMIT = 56 * 2**20
ACC_LIMIT = 49 * 2**20
HIGHEST = lax.Precision.HIGHEST
PIVOTS = 8
ANY = pl.BlockSpec(memory_space=pl.ANY)
WHOLE = pl.BlockSpec(memory_space=pltpu.VMEM)


def params(limit=VMEM_LIMIT):
    return pltpu.CompilerParams(vmem_limit_bytes=limit)


def split(value):
    high = value.astype(jnp.bfloat16)
    rest = value - high.astype(jnp.float32)
    middle = rest.astype(jnp.bfloat16)
    low = (rest - middle.astype(jnp.float32)).astype(jnp.bfloat16)
    return high, middle, low


def add_parts(product):
    return product[:RANK] + (product[RANK : 2 * RANK] + product[2 * RANK :])


def whole_copies(sources, targets, sems):
    return [
        pltpu.make_async_copy(source, target, sems.at[i])
        for i, (source, target) in enumerate(zip(sources, targets))
    ]


def left_kernel(
    act_hbm, grad_hbm, error_hbm, right_hbm, left_ref,
    act_ref, grad_ref, error_ref, right_ref, sems,
):
    act_copy, grad_copy, error_copy, right_copy = whole_copies(
        (act_hbm, grad_hbm, error_hbm, right_hbm),
        (act_ref, grad_ref, error_ref, right_ref),
        sems,
    )
    right_copy.start()
    grad_copy.start()
    act_copy.start()
    error_copy.start()
    right_copy.wait()
    grad_copy.wait()
    inner = jnp.dot(right_ref[...], grad_ref[...], preferred_element_type=jnp.float32)
    parts = jnp.concatenate(split(inner), axis=0)
    act_copy.wait()
    total = add_parts(jnp.dot(parts, act_ref[...], preferred_element_type=jnp.float32))
    error_copy.wait()
    total = total + jnp.dot(right_ref[...], error_ref[...], preferred_element_type=jnp.float32)
    for tile in range(ROW_TILES):
        left_ref[pl.ds(tile * RANK, RANK), :] = total[:, tile * LANES : (tile + 1) * LANES]


def left_term(act, grad, error, right):
    return pl.pallas_call(
        left_kernel,
        in_specs=[ANY] * 4,
        out_specs=WHOLE,
        out_shape=jax.ShapeDtypeStruct((ROW_TILES * RANK, LANES), jnp.float32),
        scratch_shapes=[
            pltpu.VMEM((TOK, ROWS), jnp.bfloat16),
            pltpu.VMEM((COLS, TOK), jnp.bfloat16),
            pltpu.VMEM((COLS, ROWS), jnp.bfloat16),
            pltpu.VMEM((RANK, COLS), jnp.bfloat16),
            pltpu.SemaphoreType.DMA((4,)),
        ],
        compiler_params=params(LEFT_LIMIT),
        cost_estimate=pl.CostEstimate(
            flops=2 * RANK * (COLS * (ROWS + TOK) + ROWS * TOK),
            bytes_accessed=9_000_000, transcendentals=0,
        ),
        name="left_term",
    )(act, grad, error, right)


def accumulate_kernel(
    half, act_hbm, grad_hbm, error_hbm, acc_ref,
    act_ref, grad_ref, error_ref, sems, grad_sems, error_sems,
):
    chunks = [(i, a, n) for i, (h, a, n) in enumerate(c for c in CHUNKS if c[0] == half)]
    act_copy = pltpu.make_async_copy(act_hbm, act_ref, sems.at[0])
    grad_copies, error_copies = [], []
    act_copy.start()
    for i, a, n in chunks:
        here, there = pl.ds(a, n), pl.ds(half * HALF + a, n)
        grad_copies.append(
            pltpu.make_async_copy(grad_hbm.at[there], grad_ref.at[here], grad_sems.at[i])
        )
        error_copies.append(
            pltpu.make_async_copy(error_hbm.at[there], error_ref.at[here], error_sems.at[i])
        )
        grad_copies[i].start()
        error_copies[i].start()
    act_copy.wait()
    for i, a, n in chunks:
        rows = pl.ds(a, n)
        grad_copies[i].wait()
        gradient = jnp.dot(grad_ref[rows, :], act_ref[...], preferred_element_type=jnp.float32)
        error_copies[i].wait()
        acc_ref[rows, :] = (error_ref[rows, :].astype(jnp.float32) + gradient).astype(jnp.bfloat16)


def accumulate(half, act, grad, error):
    size = HALVES[half]
    return pl.pallas_call(
        functools.partial(accumulate_kernel, half),
        in_specs=[ANY] * 3,
        out_specs=WHOLE,
        out_shape=jax.ShapeDtypeStruct((size, ROWS), jnp.bfloat16),
        scratch_shapes=[
            pltpu.VMEM((TOK, ROWS), jnp.bfloat16),
            pltpu.VMEM((size, TOK), jnp.bfloat16),
            pltpu.VMEM((size, ROWS), jnp.bfloat16),
            pltpu.SemaphoreType.DMA((1,)),
            pltpu.SemaphoreType.DMA((2,)),
            pltpu.SemaphoreType.DMA((2,)),
        ],
        compiler_params=params(ACC_LIMIT),
        cost_estimate=pl.CostEstimate(
            flops=2 * size * ROWS * TOK, bytes_accessed=8_000_000, transcendentals=0
        ),
        name="accumulate",
    )(act, grad, error)


def project_kernel(left_ref, acc_a, acc_b, out_ref, parts_ref):
    acc = (acc_a, acc_b)
    for tile in range(ROW_TILES):
        lanes = pl.ds(tile * LANES, LANES)
        mean = left_ref[pl.ds(tile * RANK, RANK), :] * (1.0 / N_DP)
        for i, part in enumerate(split(mean)):
            parts_ref[pl.ds(i * RANK, RANK), lanes] = part
    parts = parts_ref[...]
    for i, (h, a, n) in enumerate(CHUNKS):
        product = lax.dot_general(
            parts, acc[h][pl.ds(a, n), :], (((1,), (1,)), ((), ())),
            preferred_element_type=jnp.float32,
        )
        total = add_parts(product)
        for tile in range(-(-n // LANES)):
            piece = total[:, tile * LANES : min(n, (tile + 1) * LANES)]
            spare = LANES - piece.shape[1]
            if spare:
                piece = jnp.concatenate([piece, jnp.zeros((RANK, spare), jnp.float32)], axis=1)
            out_ref[pl.ds(((h * HALF + a) // LANES + tile) * RANK, RANK), :] = piece


def project(left_sum, acc_a, acc_b):
    return pl.pallas_call(
        project_kernel,
        in_specs=[WHOLE] * 3,
        out_specs=WHOLE,
        out_shape=jax.ShapeDtypeStruct((COL_TILES * RANK, LANES), jnp.float32),
        scratch_shapes=[pltpu.VMEM((3 * RANK, ROWS), jnp.bfloat16)],
        compiler_params=params(32 * 2**20),
        cost_estimate=pl.CostEstimate(
            flops=6 * COLS * ROWS * RANK, bytes_accessed=4_500_000, transcendentals=0
        ),
        name="project",
    )(left_sum, acc_a, acc_b)


def eliminate(gram):
    row = lax.broadcasted_iota(jnp.int32, (RANK, 2 * RANK), 0)
    lane = lax.broadcasted_iota(jnp.int32, (RANK, 2 * RANK), 1)
    unit = jnp.where(lane == row + RANK, 1.0, 0.0)
    work = jnp.where(lane < RANK, jnp.concatenate([gram, gram], axis=1), unit)
    for start in range(0, RANK, PIVOTS):
        columns = [
            jnp.broadcast_to(work[:, start + j : start + j + 1], (RANK, 2 * RANK))
            for j in range(PIVOTS)
        ]
        rows = [work[start + j : start + j + 1, :] for j in range(PIVOTS)]
        square = [
            [columns[m][start + j : start + j + 1, :] for m in range(PIVOTS)]
            for j in range(PIVOTS)
        ]
        update = None
        for j in range(PIVOTS):
            scale = 1.0 / square[j][j]
            for i in range(j + 1, PIVOTS):
                factor = square[i][j] * scale
                rows[i] = rows[i] - factor * rows[j]
                for m in range(j + 1, PIVOTS):
                    square[i][m] = square[i][m] - factor * square[j][m]
            factor = columns[j] * scale
            for m in range(j + 1, PIVOTS):
                columns[m] = columns[m] - factor * square[j][m]
            term = factor * rows[j]
            update = term if update is None else update + term
        work = jnp.where(row >= start + PIVOTS, work - update, work)
        for j in range(PIVOTS):
            done = rows[j] * (1.0 / jnp.sqrt(square[j][j]))
            work = jnp.where(row == start + j, done, work)
    return work[:, RANK:]


def orthonormal_kernel(left_ref, inverse_ref, out_ref):
    mean = jnp.concatenate(
        [left_ref[pl.ds(tile * RANK, RANK), :] for tile in range(ROW_TILES)], axis=1
    ) * (1.0 / N_DP)
    gram = lax.dot_general(
        mean, mean, (((1,), (1,)), ((), ())),
        precision=HIGHEST, preferred_element_type=jnp.float32,
    )
    inverse = eliminate(gram)
    inverse_ref[...] = inverse
    out_ref[...] = jnp.dot(inverse, mean, precision=HIGHEST, preferred_element_type=jnp.float32)


def orthonormal(left_sum):
    return pl.pallas_call(
        orthonormal_kernel,
        in_specs=[WHOLE],
        out_specs=[WHOLE, WHOLE],
        out_shape=[
            jax.ShapeDtypeStruct((RANK, RANK), jnp.float32),
            jax.ShapeDtypeStruct((RANK, ROWS), jnp.float32),
        ],
        compiler_params=params(16 * 2**20),
        cost_estimate=pl.CostEstimate(
            flops=40_000_000, bytes_accessed=600_000, transcendentals=0
        ),
        name="orthonormal",
    )(left_sum)


def finish_kernel(
    sum_ref, inverse_ref, left_ref, acc_a, acc_b, left_hbm, right_hbm, error_hbm,
    right_ref, error_ref, out_sems, error_sems,
):
    acc = (acc_a, acc_b)
    starts = [h * HALF + a for h, a, n in CHUNKS]
    error_copies = [
        pltpu.make_async_copy(
            error_ref.at[pl.ds(start, chunk[2])],
            error_hbm.at[pl.ds(start, chunk[2])],
            error_sems.at[i],
        )
        for i, (start, chunk) in enumerate(zip(starts, CHUNKS))
    ]
    left_copy = pltpu.make_async_copy(left_ref, left_hbm, out_sems.at[0])
    right_copy = pltpu.make_async_copy(right_ref, right_hbm, out_sems.at[1])
    terms = jnp.concatenate(
        [sum_ref[pl.ds(tile * RANK, RANK), :] for tile in range(COL_TILES)], axis=1
    )
    right = jnp.dot(
        inverse_ref[...], terms, precision=HIGHEST, preferred_element_type=jnp.float32
    )
    right = (right * (1.0 / N_DP)).astype(jnp.bfloat16)
    right_ref[...] = right[:, :COLS]
    left_copy.start()
    right_copy.start()
    left = left_ref[...].astype(jnp.bfloat16)
    for i, (h, a, n) in enumerate(CHUNKS):
        start = starts[i]
        update = lax.dot_general(
            right_ref[:, start : start + n], left, (((0,), (0,)), ((), ())),
            preferred_element_type=jnp.float32,
        )
        held = acc[h][pl.ds(a, n), :].astype(jnp.float32)
        error_ref[pl.ds(start, n), :] = (held - update).astype(jnp.bfloat16)
        error_copies[i].start()
    left_copy.wait()
    right_copy.wait()
    for copy in error_copies:
        copy.wait()


def finish(right_sum, inverse, left, acc_a, acc_b):
    return pl.pallas_call(
        finish_kernel,
        in_specs=[WHOLE] * 5,
        out_specs=[ANY, ANY, ANY],
        out_shape=[
            jax.ShapeDtypeStruct((RANK, ROWS), jnp.float32),
            jax.ShapeDtypeStruct((RANK, COLS), jnp.bfloat16),
            jax.ShapeDtypeStruct((COLS, ROWS), jnp.bfloat16),
        ],
        scratch_shapes=[
            pltpu.VMEM((RANK, COLS), jnp.bfloat16),
            pltpu.VMEM((COLS, ROWS), jnp.bfloat16),
            pltpu.SemaphoreType.DMA((2,)),
            pltpu.SemaphoreType.DMA((len(CHUNKS),)),
        ],
        compiler_params=params(32 * 2**20),
        cost_estimate=pl.CostEstimate(
            flops=2 * COLS * ROWS * RANK, bytes_accessed=8_500_000, transcendentals=0
        ),
        name="finish",
    )(right_sum, inverse, left, acc_a, acc_b)


def exchange(pieces, axes):
    return lax.all_to_all(pieces, axes, 0, 0, tiled=True)


def spread(total, count):
    return jnp.broadcast_to(total[None], (count,) + total.shape)


def sum_left(part, first, second):
    mine = jnp.sum(exchange(part.reshape(32, 16, LANES), PLANE), axis=0)
    mine, first = lax.optimization_barrier((mine, first))
    mine = jnp.sum(exchange(spread(mine, 8), Z), axis=0)
    total = exchange(spread(mine, 32), PLANE).reshape(part.shape)
    return total, (first, second)


def sum_right(part, work):
    mine = jnp.sum(exchange(part.reshape(8, 120, LANES), NEAR), axis=0)
    mine, work = lax.optimization_barrier((mine, work))
    mine = jnp.sum(exchange(spread(mine, 4), "zh"), axis=0)
    return exchange(spread(mine, 8), NEAR).reshape(part.shape), work


def local(activations, output_grads, error_buffer, right_start):
    grad, error = output_grads.T, error_buffer[0].T
    left_part = left_term(activations, grad, error, right_start.T)
    acc = [accumulate(half, activations, grad, error) for half in range(2)]
    left_sum, acc = sum_left(left_part, *acc)
    right_part = project(left_sum, *acc)
    right_sum, (inverse, left) = sum_right(right_part, orthonormal(left_sum))
    left_factor, right_factor, new_error = finish(right_sum, inverse, left, *acc)
    return (left_factor.T, right_factor.T, new_error.T[None])


def solution(mesh):
    fine = Mesh(mesh.devices.reshape(4, 4, 2, 4, 2), DP + ("y", "core"))
    tensor = ("y", "core")
    return jax.shard_map(
        local,
        mesh=fine,
        in_specs=(P(DP, None), P(DP, tensor), P(DP, None, tensor), P(tensor, None)),
        out_specs=(P(), P(tensor, None), P(DP, None, tensor)),
        check_vma=False,
    )
```

```python
import functools

import jax
import jax.numpy as jnp
from jax import lax
from jax.experimental import pallas as pl
from jax.experimental.pallas import tpu as pltpu
from jax.sharding import Mesh, PartitionSpec as P

ROWS, COLS, RANK, TOK, N_DP = 1024, 1848, 64, 896, 32
LANES = 128
ROW_TILES = ROWS // LANES
COL_TILES = -(-COLS // LANES)
HALF = 640
HALVES = (HALF, COLS - HALF)
SPARE_ROWS = 12288
CHUNKS = ((1, 0, 640), (1, 640, COLS - HALF - 640), (0, 0, 384), (0, 384, HALF - 384))
Z = ("zh", "zl")
DP = ("x",) + Z
NEAR = ("x", "zl")
PLANE = ("x", "y", "core")
VMEM_LIMIT = 32 * 2**20
LEFT_LIMIT = 56 * 2**20
ACC_LIMITS = (56 * 2**20, 49 * 2**20 + 2**19)
HIGHEST = lax.Precision.HIGHEST
PIVOTS = 8
ANY = pl.BlockSpec(memory_space=pl.ANY)
WHOLE = pl.BlockSpec(memory_space=pltpu.VMEM)


def params(limit=VMEM_LIMIT):
    return pltpu.CompilerParams(vmem_limit_bytes=limit)


def split(value):
    high = value.astype(jnp.bfloat16)
    rest = value - high.astype(jnp.float32)
    middle = rest.astype(jnp.bfloat16)
    low = (rest - middle.astype(jnp.float32)).astype(jnp.bfloat16)
    return high, middle, low


def add_parts(product):
    return product[:RANK] + (product[RANK : 2 * RANK] + product[2 * RANK :])


def whole_copies(sources, targets, sems):
    return [
        pltpu.make_async_copy(source, target, sems.at[i])
        for i, (source, target) in enumerate(zip(sources, targets))
    ]


def left_kernel(
    act_hbm, grad_hbm, error_hbm, right_hbm, left_ref,
    act_ref, grad_ref, error_ref, right_ref, sems,
):
    act_copy, grad_copy, error_copy, right_copy = whole_copies(
        (act_hbm, grad_hbm, error_hbm, right_hbm),
        (act_ref, grad_ref, error_ref, right_ref),
        sems,
    )
    right_copy.start()
    grad_copy.start()
    act_copy.start()
    error_copy.start()
    right_copy.wait()
    grad_copy.wait()
    inner = jnp.dot(right_ref[...], grad_ref[...], preferred_element_type=jnp.float32)
    parts = jnp.concatenate(split(inner), axis=0)
    act_copy.wait()
    total = add_parts(jnp.dot(parts, act_ref[...], preferred_element_type=jnp.float32))
    error_copy.wait()
    total = total + jnp.dot(right_ref[...], error_ref[...], preferred_element_type=jnp.float32)
    for tile in range(ROW_TILES):
        left_ref[pl.ds(tile * RANK, RANK), :] = total[:, tile * LANES : (tile + 1) * LANES]


def left_term(act, grad, error, right):
    return pl.pallas_call(
        left_kernel,
        in_specs=[ANY] * 4,
        out_specs=WHOLE,
        out_shape=jax.ShapeDtypeStruct((ROW_TILES * RANK, LANES), jnp.float32),
        scratch_shapes=[
            pltpu.VMEM((TOK, ROWS), jnp.bfloat16),
            pltpu.VMEM((COLS, TOK), jnp.bfloat16),
            pltpu.VMEM((COLS, ROWS), jnp.bfloat16),
            pltpu.VMEM((RANK, COLS), jnp.bfloat16),
            pltpu.SemaphoreType.DMA((4,)),
        ],
        compiler_params=params(LEFT_LIMIT),
        cost_estimate=pl.CostEstimate(
            flops=2 * RANK * (COLS * (ROWS + TOK) + ROWS * TOK),
            bytes_accessed=9_000_000, transcendentals=0,
        ),
        name="left_term",
    )(act, grad, error, right)


def accumulate_kernel(
    half, act_hbm, grad_hbm, error_hbm, out_ref,
    act_ref, grad_ref, error_ref, sems, grad_sems, error_sems, *spare
):
    chunks = [(i, a, n) for i, (h, a, n) in enumerate(c for c in CHUNKS if c[0] == half)]
    act_copy = pltpu.make_async_copy(act_hbm, act_ref, sems.at[0])
    grad_copies, error_copies, acc_copies = [], [], []
    acc_ref = spare[0] if spare else out_ref
    act_copy.start()
    for i, a, n in chunks:
        here, there = pl.ds(a, n), pl.ds(half * HALF + a, n)
        grad_copies.append(
            pltpu.make_async_copy(grad_hbm.at[there], grad_ref.at[here], grad_sems.at[i])
        )
        error_copies.append(
            pltpu.make_async_copy(error_hbm.at[there], error_ref.at[here], error_sems.at[i])
        )
        if spare:
            acc_copies.append(
                pltpu.make_async_copy(acc_ref.at[here], out_ref.at[here], spare[1].at[i])
            )
        grad_copies[i].start()
        error_copies[i].start()
    act_copy.wait()
    for i, a, n in chunks:
        rows = pl.ds(a, n)
        grad_copies[i].wait()
        gradient = jnp.dot(grad_ref[rows, :], act_ref[...], preferred_element_type=jnp.float32)
        error_copies[i].wait()
        acc_ref[rows, :] = (error_ref[rows, :].astype(jnp.float32) + gradient).astype(jnp.bfloat16)
        if spare:
            acc_copies[i].start()
    for copy in acc_copies:
        copy.wait()


def accumulate(half, act, grad, error):
    size = HALVES[half]
    spare = [pltpu.VMEM((size, ROWS), jnp.bfloat16), pltpu.SemaphoreType.DMA((2,))]
    return pl.pallas_call(
        functools.partial(accumulate_kernel, half),
        in_specs=[ANY] * 3,
        out_specs=WHOLE if half else ANY,
        out_shape=jax.ShapeDtypeStruct((size if half else SPARE_ROWS, ROWS), jnp.bfloat16),
        scratch_shapes=[
            pltpu.VMEM((TOK, ROWS), jnp.bfloat16),
            pltpu.VMEM((size, TOK), jnp.bfloat16),
            pltpu.VMEM((size, ROWS), jnp.bfloat16),
            pltpu.SemaphoreType.DMA((1,)),
            pltpu.SemaphoreType.DMA((2,)),
            pltpu.SemaphoreType.DMA((2,)),
        ]
        + spare * (1 - half),
        compiler_params=params(ACC_LIMITS[half]),
        cost_estimate=pl.CostEstimate(
            flops=2 * size * ROWS * TOK, bytes_accessed=8_000_000, transcendentals=0
        ),
        name="accumulate",
    )(act, grad, error)


def first_half(source, target, sems):
    return {
        i: pltpu.make_async_copy(source.at[pl.ds(a, n)], target.at[pl.ds(a, n)], sems.at[i])
        for i, (h, a, n) in enumerate(CHUNKS)
        if h == 0
    }


def project_kernel(left_ref, acc_a, acc_b, out_ref, parts_ref, half_a, sems):
    acc = (half_a, acc_b)
    copies = first_half(acc_a, half_a, sems)
    for copy in copies.values():
        copy.start()
    for tile in range(ROW_TILES):
        lanes = pl.ds(tile * LANES, LANES)
        mean = left_ref[pl.ds(tile * RANK, RANK), :] * (1.0 / N_DP)
        for i, part in enumerate(split(mean)):
            parts_ref[pl.ds(i * RANK, RANK), lanes] = part
    parts = parts_ref[...]
    for i, (h, a, n) in enumerate(CHUNKS):
        if i in copies:
            copies[i].wait()
        product = lax.dot_general(
            parts, acc[h][pl.ds(a, n), :], (((1,), (1,)), ((), ())),
            preferred_element_type=jnp.float32,
        )
        total = add_parts(product)
        for tile in range(-(-n // LANES)):
            piece = total[:, tile * LANES : min(n, (tile + 1) * LANES)]
            spare = LANES - piece.shape[1]
            if spare:
                piece = jnp.concatenate([piece, jnp.zeros((RANK, spare), jnp.float32)], axis=1)
            out_ref[pl.ds(((h * HALF + a) // LANES + tile) * RANK, RANK), :] = piece


def project(left_sum, acc_a, acc_b):
    return pl.pallas_call(
        project_kernel,
        in_specs=[WHOLE, ANY, WHOLE],
        out_specs=WHOLE,
        out_shape=jax.ShapeDtypeStruct((COL_TILES * RANK, LANES), jnp.float32),
        scratch_shapes=[
            pltpu.VMEM((3 * RANK, ROWS), jnp.bfloat16),
            pltpu.VMEM((HALVES[0], ROWS), jnp.bfloat16),
            pltpu.SemaphoreType.DMA((len(CHUNKS),)),
        ],
        compiler_params=params(),
        cost_estimate=pl.CostEstimate(
            flops=6 * COLS * ROWS * RANK, bytes_accessed=4_500_000, transcendentals=0
        ),
        name="project",
    )(left_sum, acc_a, acc_b)


def eliminate(gram):
    row = lax.broadcasted_iota(jnp.int32, (RANK, 2 * RANK), 0)
    lane = lax.broadcasted_iota(jnp.int32, (RANK, 2 * RANK), 1)
    unit = jnp.where(lane == row + RANK, 1.0, 0.0)
    work = jnp.where(lane < RANK, jnp.concatenate([gram, gram], axis=1), unit)
    for start in range(0, RANK, PIVOTS):
        columns = [
            jnp.broadcast_to(work[:, start + j : start + j + 1], (RANK, 2 * RANK))
            for j in range(PIVOTS)
        ]
        rows = [work[start + j : start + j + 1, :] for j in range(PIVOTS)]
        square = [
            [columns[m][start + j : start + j + 1, :] for m in range(PIVOTS)]
            for j in range(PIVOTS)
        ]
        update = None
        for j in range(PIVOTS):
            scale = 1.0 / square[j][j]
            for i in range(j + 1, PIVOTS):
                factor = square[i][j] * scale
                rows[i] = rows[i] - factor * rows[j]
                for m in range(j + 1, PIVOTS):
                    square[i][m] = square[i][m] - factor * square[j][m]
            factor = columns[j] * scale
            for m in range(j + 1, PIVOTS):
                columns[m] = columns[m] - factor * square[j][m]
            term = factor * rows[j]
            update = term if update is None else update + term
        work = jnp.where(row >= start + PIVOTS, work - update, work)
        for j in range(PIVOTS):
            done = rows[j] * (1.0 / jnp.sqrt(square[j][j]))
            work = jnp.where(row == start + j, done, work)
    return work[:, RANK:]


def orthonormal_kernel(left_ref, inverse_ref, out_ref):
    mean = jnp.concatenate(
        [left_ref[pl.ds(tile * RANK, RANK), :] for tile in range(ROW_TILES)], axis=1
    ) * (1.0 / N_DP)
    gram = lax.dot_general(
        mean, mean, (((1,), (1,)), ((), ())),
        precision=HIGHEST, preferred_element_type=jnp.float32,
    )
    inverse = eliminate(gram)
    inverse_ref[...] = inverse
    out_ref[...] = jnp.dot(inverse, mean, precision=HIGHEST, preferred_element_type=jnp.float32)


def orthonormal(left_sum):
    return pl.pallas_call(
        orthonormal_kernel,
        in_specs=[WHOLE],
        out_specs=[WHOLE, WHOLE],
        out_shape=[
            jax.ShapeDtypeStruct((RANK, RANK), jnp.float32),
            jax.ShapeDtypeStruct((RANK, ROWS), jnp.float32),
        ],
        compiler_params=params(16 * 2**20),
        cost_estimate=pl.CostEstimate(
            flops=40_000_000, bytes_accessed=600_000, transcendentals=0
        ),
        name="orthonormal",
    )(left_sum)


def finish_kernel(
    sum_ref, inverse_ref, left_ref, acc_a, acc_b, left_hbm, right_hbm, error_hbm,
    half_a, right_ref, error_ref, sems, out_sems, error_sems,
):
    acc = (half_a, acc_b)
    copies = first_half(acc_a, half_a, sems)
    for copy in copies.values():
        copy.start()
    starts = [h * HALF + a for h, a, n in CHUNKS]
    error_copies = [
        pltpu.make_async_copy(
            error_ref.at[pl.ds(start, chunk[2])],
            error_hbm.at[pl.ds(start, chunk[2])],
            error_sems.at[i],
        )
        for i, (start, chunk) in enumerate(zip(starts, CHUNKS))
    ]
    left_copy = pltpu.make_async_copy(left_ref, left_hbm, out_sems.at[0])
    right_copy = pltpu.make_async_copy(right_ref, right_hbm, out_sems.at[1])
    terms = jnp.concatenate(
        [sum_ref[pl.ds(tile * RANK, RANK), :] for tile in range(COL_TILES)], axis=1
    )
    right = jnp.dot(
        inverse_ref[...], terms, precision=HIGHEST, preferred_element_type=jnp.float32
    )
    right = (right * (1.0 / N_DP)).astype(jnp.bfloat16)
    right_ref[...] = right[:, :COLS]
    left_copy.start()
    right_copy.start()
    left = left_ref[...].astype(jnp.bfloat16)
    for i, (h, a, n) in enumerate(CHUNKS):
        start = starts[i]
        update = lax.dot_general(
            right_ref[:, start : start + n], left, (((0,), (0,)), ((), ())),
            preferred_element_type=jnp.float32,
        )
        if i in copies:
            copies[i].wait()
        held = acc[h][pl.ds(a, n), :].astype(jnp.float32)
        error_ref[pl.ds(start, n), :] = (held - update).astype(jnp.bfloat16)
        error_copies[i].start()
    left_copy.wait()
    right_copy.wait()
    for copy in error_copies:
        copy.wait()


def finish(right_sum, inverse, left, acc_a, acc_b):
    return pl.pallas_call(
        finish_kernel,
        in_specs=[WHOLE] * 3 + [ANY, WHOLE],
        out_specs=[ANY, ANY, ANY],
        out_shape=[
            jax.ShapeDtypeStruct((RANK, ROWS), jnp.float32),
            jax.ShapeDtypeStruct((RANK, COLS), jnp.bfloat16),
            jax.ShapeDtypeStruct((COLS, ROWS), jnp.bfloat16),
        ],
        scratch_shapes=[
            pltpu.VMEM((HALVES[0], ROWS), jnp.bfloat16),
            pltpu.VMEM((RANK, COLS), jnp.bfloat16),
            pltpu.VMEM((COLS, ROWS), jnp.bfloat16),
            pltpu.SemaphoreType.DMA((len(CHUNKS),)),
            pltpu.SemaphoreType.DMA((2,)),
            pltpu.SemaphoreType.DMA((len(CHUNKS),)),
        ],
        compiler_params=params(),
        cost_estimate=pl.CostEstimate(
            flops=2 * COLS * ROWS * RANK, bytes_accessed=8_500_000, transcendentals=0
        ),
        name="finish",
    )(right_sum, inverse, left, acc_a, acc_b)


def exchange(pieces, axes):
    return lax.all_to_all(pieces, axes, 0, 0, tiled=True)


def spread(total, count):
    return jnp.broadcast_to(total[None], (count,) + total.shape)


def sum_left(part, first, second):
    mine = jnp.sum(exchange(part.reshape(32, 16, LANES), PLANE), axis=0)
    mine, first = lax.optimization_barrier((mine, first))
    mine = jnp.sum(exchange(spread(mine, 8), Z), axis=0)
    total = exchange(spread(mine, 32), PLANE).reshape(part.shape)
    return total, (first, second)


def sum_right(part, work):
    mine = jnp.sum(exchange(part.reshape(8, 120, LANES), NEAR), axis=0)
    mine, work = lax.optimization_barrier((mine, work))
    mine = jnp.sum(exchange(spread(mine, 4), "zh"), axis=0)
    return exchange(spread(mine, 8), NEAR).reshape(part.shape), work


def local(activations, output_grads, error_buffer, right_start):
    grad, error = output_grads.T, error_buffer[0].T
    left_part = left_term(activations, grad, error, right_start.T)
    acc = [accumulate(half, activations, grad, error) for half in range(2)]
    left_sum, acc = sum_left(left_part, *acc)
    right_part = project(left_sum, *acc)
    right_sum, (inverse, left) = sum_right(right_part, orthonormal(left_sum))
    left_factor, right_factor, new_error = finish(right_sum, inverse, left, *acc)
    return (left_factor.T, right_factor.T, new_error.T[None])


def solution(mesh):
    fine = Mesh(mesh.devices.reshape(4, 4, 2, 4, 2), DP + ("y", "core"))
    tensor = ("y", "core")
    return jax.shard_map(
        local,
        mesh=fine,
        in_specs=(P(DP, None), P(DP, tensor), P(DP, None, tensor), P(tensor, None)),
        out_specs=(P(), P(tensor, None), P(DP, None, tensor)),
        check_vma=False,
    )
```

```python
import functools

import jax
import jax.numpy as jnp
from jax import lax
from jax.experimental import pallas as pl
from jax.experimental.pallas import tpu as pltpu
from jax.sharding import Mesh, PartitionSpec as P

ROWS, COLS, RANK, TOK, N_DP = 1024, 1848, 64, 896, 32
LANES = 128
ROW_TILES = ROWS // LANES
COL_TILES = -(-COLS // LANES)
HALF = 640
HALVES = (HALF, COLS - HALF)
SPARE_ROWS = 12288
CHUNKS = ((1, 0, 640), (1, 640, COLS - HALF - 640), (0, 0, 384), (0, 384, HALF - 384))
Z = ("zh", "zl")
DP = ("x",) + Z
NEAR = ("x", "zl")
PLANE = ("x", "y", "core")
VMEM_LIMIT = 32 * 2**20
LEFT_LIMIT = 56 * 2**20
ACC_LIMITS = (56 * 2**20, 49 * 2**20 + 2**19)
HIGHEST = lax.Precision.HIGHEST
PIVOTS = 8
ANY = pl.BlockSpec(memory_space=pl.ANY)
WHOLE = pl.BlockSpec(memory_space=pltpu.VMEM)


def params(limit=VMEM_LIMIT):
    return pltpu.CompilerParams(vmem_limit_bytes=limit)


def split(value):
    high = value.astype(jnp.bfloat16)
    return high, (value - high.astype(jnp.float32)).astype(jnp.bfloat16)


def add_parts(product):
    return product[:RANK] + product[RANK:]


def whole_copies(sources, targets, sems):
    return [
        pltpu.make_async_copy(source, target, sems.at[i])
        for i, (source, target) in enumerate(zip(sources, targets))
    ]


def left_kernel(
    act_hbm, grad_hbm, error_hbm, right_hbm, left_ref,
    act_ref, grad_ref, error_ref, right_ref, sems,
):
    act_copy, grad_copy, error_copy, right_copy = whole_copies(
        (act_hbm, grad_hbm, error_hbm, right_hbm),
        (act_ref, grad_ref, error_ref, right_ref),
        sems,
    )
    right_copy.start()
    grad_copy.start()
    act_copy.start()
    error_copy.start()
    right_copy.wait()
    grad_copy.wait()
    inner = jnp.dot(right_ref[...], grad_ref[...], preferred_element_type=jnp.float32)
    parts = jnp.concatenate(split(inner), axis=0)
    act_copy.wait()
    total = add_parts(jnp.dot(parts, act_ref[...], preferred_element_type=jnp.float32))
    error_copy.wait()
    total = total + jnp.dot(right_ref[...], error_ref[...], preferred_element_type=jnp.float32)
    for tile in range(ROW_TILES):
        left_ref[pl.ds(tile * RANK, RANK), :] = total[:, tile * LANES : (tile + 1) * LANES]


def left_term(act, grad, error, right):
    return pl.pallas_call(
        left_kernel,
        in_specs=[ANY] * 4,
        out_specs=WHOLE,
        out_shape=jax.ShapeDtypeStruct((ROW_TILES * RANK, LANES), jnp.float32),
        scratch_shapes=[
            pltpu.VMEM((TOK, ROWS), jnp.bfloat16),
            pltpu.VMEM((COLS, TOK), jnp.bfloat16),
            pltpu.VMEM((COLS, ROWS), jnp.bfloat16),
            pltpu.VMEM((RANK, COLS), jnp.bfloat16),
            pltpu.SemaphoreType.DMA((4,)),
        ],
        compiler_params=params(LEFT_LIMIT),
        cost_estimate=pl.CostEstimate(
            flops=2 * RANK * (COLS * (ROWS + TOK) + ROWS * TOK),
            bytes_accessed=9_000_000, transcendentals=0,
        ),
        name="left_term",
    )(act, grad, error, right)


def accumulate_kernel(
    half, act_hbm, grad_hbm, error_hbm, out_ref,
    act_ref, grad_ref, error_ref, sems, grad_sems, error_sems, *spare
):
    chunks = [(i, a, n) for i, (h, a, n) in enumerate(c for c in CHUNKS if c[0] == half)]
    act_copy = None if half else pltpu.make_async_copy(act_hbm, act_ref, sems.at[0])
    act_ref = act_hbm if half else act_ref
    grad_copies, error_copies, acc_copies = [], [], []
    acc_ref = spare[0] if spare else out_ref
    if act_copy:
        act_copy.start()
    for i, a, n in chunks:
        here, there = pl.ds(a, n), pl.ds(half * HALF + a, n)
        grad_copies.append(
            pltpu.make_async_copy(grad_hbm.at[there], grad_ref.at[here], grad_sems.at[i])
        )
        error_copies.append(
            pltpu.make_async_copy(error_hbm.at[there], error_ref.at[here], error_sems.at[i])
        )
        if spare:
            acc_copies.append(
                pltpu.make_async_copy(acc_ref.at[here], out_ref.at[here], spare[1].at[i])
            )
    grad_copies[0].start()
    error_copies[0].start()
    if act_copy:
        act_copy.wait()
    for i, a, n in chunks:
        rows = pl.ds(a, n)
        grad_copies[i].wait()
        if i + 1 < len(chunks):
            grad_copies[i + 1].start()
            error_copies[i + 1].start()
        gradient = jnp.dot(grad_ref[rows, :], act_ref[...], preferred_element_type=jnp.float32)
        error_copies[i].wait()
        acc_ref[rows, :] = (error_ref[rows, :].astype(jnp.float32) + gradient).astype(jnp.bfloat16)
        if spare:
            acc_copies[i].start()
    for copy in acc_copies:
        copy.wait()


def accumulate(half, act, grad, error):
    size = HALVES[half]
    spare = [pltpu.VMEM((size, ROWS), jnp.bfloat16), pltpu.SemaphoreType.DMA((2,))]
    return pl.pallas_call(
        functools.partial(accumulate_kernel, half),
        in_specs=[WHOLE if half else ANY, ANY, ANY],
        out_specs=WHOLE if half else ANY,
        out_shape=jax.ShapeDtypeStruct((size if half else SPARE_ROWS, ROWS), jnp.bfloat16),
        scratch_shapes=[
            pltpu.VMEM((TOK if half == 0 else 16, ROWS), jnp.bfloat16),
            pltpu.VMEM((size, TOK), jnp.bfloat16),
            pltpu.VMEM((size, ROWS), jnp.bfloat16),
            pltpu.SemaphoreType.DMA((1,)),
            pltpu.SemaphoreType.DMA((2,)),
            pltpu.SemaphoreType.DMA((2,)),
        ]
        + spare * (1 - half),
        compiler_params=params(ACC_LIMITS[half]),
        cost_estimate=pl.CostEstimate(
            flops=2 * size * ROWS * TOK, bytes_accessed=8_000_000, transcendentals=0
        ),
        name="accumulate",
    )(act, grad, error)


def first_half(source, target, sems):
    return {
        i: pltpu.make_async_copy(source.at[pl.ds(a, n)], target.at[pl.ds(a, n)], sems.at[i])
        for i, (h, a, n) in enumerate(CHUNKS)
        if h == 0
    }


def project_kernel(left_ref, acc_a, acc_b, out_ref, parts_ref, half_a, sems):
    acc = (half_a, acc_b)
    copies = first_half(acc_a, half_a, sems)
    for copy in copies.values():
        copy.start()
    for tile in range(ROW_TILES):
        lanes = pl.ds(tile * LANES, LANES)
        mean = left_ref[pl.ds(tile * RANK, RANK), :] * (1.0 / N_DP)
        for i, part in enumerate(split(mean)):
            parts_ref[pl.ds(i * RANK, RANK), lanes] = part
    parts = parts_ref[...]
    for i, (h, a, n) in enumerate(CHUNKS):
        if i in copies:
            copies[i].wait()
        product = lax.dot_general(
            parts, acc[h][pl.ds(a, n), :], (((1,), (1,)), ((), ())),
            preferred_element_type=jnp.float32,
        )
        total = add_parts(product)
        for tile in range(-(-n // LANES)):
            piece = total[:, tile * LANES : min(n, (tile + 1) * LANES)]
            spare = LANES - piece.shape[1]
            if spare:
                piece = jnp.concatenate([piece, jnp.zeros((RANK, spare), jnp.float32)], axis=1)
            out_ref[pl.ds(((h * HALF + a) // LANES + tile) * RANK, RANK), :] = piece


def project(left_sum, acc_a, acc_b):
    return pl.pallas_call(
        project_kernel,
        in_specs=[WHOLE, ANY, WHOLE],
        out_specs=WHOLE,
        out_shape=jax.ShapeDtypeStruct((COL_TILES * RANK, LANES), jnp.float32),
        scratch_shapes=[
            pltpu.VMEM((2 * RANK, ROWS), jnp.bfloat16),
            pltpu.VMEM((HALVES[0], ROWS), jnp.bfloat16),
            pltpu.SemaphoreType.DMA((len(CHUNKS),)),
        ],
        compiler_params=params(),
        cost_estimate=pl.CostEstimate(
            flops=4 * COLS * ROWS * RANK, bytes_accessed=4_500_000, transcendentals=0
        ),
        name="project",
    )(left_sum, acc_a, acc_b)


def eliminate(gram):
    row = lax.broadcasted_iota(jnp.int32, (RANK, 2 * RANK), 0)
    lane = lax.broadcasted_iota(jnp.int32, (RANK, 2 * RANK), 1)
    unit = jnp.where(lane == row + RANK, 1.0, 0.0)
    work = jnp.where(lane < RANK, jnp.concatenate([gram, gram], axis=1), unit)
    for start in range(0, RANK, PIVOTS):
        columns = [
            jnp.broadcast_to(work[:, start + j : start + j + 1], (RANK, 2 * RANK))
            for j in range(PIVOTS)
        ]
        rows = [work[start + j : start + j + 1, :] for j in range(PIVOTS)]
        square = [
            [columns[m][start + j : start + j + 1, :] for m in range(PIVOTS)]
            for j in range(PIVOTS)
        ]
        update = None
        for j in range(PIVOTS):
            scale = 1.0 / square[j][j]
            for i in range(j + 1, PIVOTS):
                factor = square[i][j] * scale
                rows[i] = rows[i] - factor * rows[j]
                for m in range(j + 1, PIVOTS):
                    square[i][m] = square[i][m] - factor * square[j][m]
            factor = columns[j] * scale
            for m in range(j + 1, PIVOTS):
                columns[m] = columns[m] - factor * square[j][m]
            term = factor * rows[j]
            update = term if update is None else update + term
        work = jnp.where(row >= start + PIVOTS, work - update, work)
        for j in range(PIVOTS):
            done = rows[j] * (1.0 / jnp.sqrt(square[j][j]))
            work = jnp.where(row == start + j, done, work)
    return work[:, RANK:]


def orthonormal_kernel(left_ref, inverse_ref, out_ref):
    mean = jnp.concatenate(
        [left_ref[pl.ds(tile * RANK, RANK), :] for tile in range(ROW_TILES)], axis=1
    ) * (1.0 / N_DP)
    gram = lax.dot_general(
        mean, mean, (((1,), (1,)), ((), ())),
        precision=HIGHEST, preferred_element_type=jnp.float32,
    )
    inverse = eliminate(gram)
    inverse_ref[...] = inverse
    out_ref[...] = jnp.dot(inverse, mean, precision=HIGHEST, preferred_element_type=jnp.float32)


def orthonormal(left_sum):
    return pl.pallas_call(
        orthonormal_kernel,
        in_specs=[WHOLE],
        out_specs=[WHOLE, WHOLE],
        out_shape=[
            jax.ShapeDtypeStruct((RANK, RANK), jnp.float32),
            jax.ShapeDtypeStruct((RANK, ROWS), jnp.float32),
        ],
        compiler_params=params(16 * 2**20),
        cost_estimate=pl.CostEstimate(
            flops=40_000_000, bytes_accessed=600_000, transcendentals=0
        ),
        name="orthonormal",
    )(left_sum)


def finish_kernel(
    sum_ref, inverse_ref, left_ref, acc_a, acc_b, left_hbm, right_hbm, error_hbm,
    half_a, right_ref, error_ref, sems, out_sems, error_sems,
):
    acc = (half_a, acc_b)
    copies = first_half(acc_a, half_a, sems)
    for copy in copies.values():
        copy.start()
    starts = [h * HALF + a for h, a, n in CHUNKS]
    error_copies = [
        pltpu.make_async_copy(
            error_ref.at[pl.ds(start, chunk[2])],
            error_hbm.at[pl.ds(start, chunk[2])],
            error_sems.at[i],
        )
        for i, (start, chunk) in enumerate(zip(starts, CHUNKS))
    ]
    left_copy = pltpu.make_async_copy(left_ref, left_hbm, out_sems.at[0])
    right_copy = pltpu.make_async_copy(right_ref, right_hbm, out_sems.at[1])
    terms = jnp.concatenate(
        [sum_ref[pl.ds(tile * RANK, RANK), :] for tile in range(COL_TILES)], axis=1
    )
    right = jnp.dot(
        inverse_ref[...], terms, precision=HIGHEST, preferred_element_type=jnp.float32
    )
    right = (right * (1.0 / N_DP)).astype(jnp.bfloat16)
    right_ref[...] = right[:, :COLS]
    left_copy.start()
    right_copy.start()
    left = left_ref[...].astype(jnp.bfloat16)
    for i, (h, a, n) in enumerate(CHUNKS):
        start = starts[i]
        update = lax.dot_general(
            right_ref[:, start : start + n], left, (((0,), (0,)), ((), ())),
            preferred_element_type=jnp.float32,
        )
        if i in copies:
            copies[i].wait()
        held = acc[h][pl.ds(a, n), :].astype(jnp.float32)
        error_ref[pl.ds(start, n), :] = (held - update).astype(jnp.bfloat16)
        error_copies[i].start()
    left_copy.wait()
    right_copy.wait()
    for copy in error_copies:
        copy.wait()


def finish(right_sum, inverse, left, acc_a, acc_b):
    return pl.pallas_call(
        finish_kernel,
        in_specs=[WHOLE] * 3 + [ANY, WHOLE],
        out_specs=[ANY, ANY, ANY],
        out_shape=[
            jax.ShapeDtypeStruct((RANK, ROWS), jnp.float32),
            jax.ShapeDtypeStruct((RANK, COLS), jnp.bfloat16),
            jax.ShapeDtypeStruct((COLS, ROWS), jnp.bfloat16),
        ],
        scratch_shapes=[
            pltpu.VMEM((HALVES[0], ROWS), jnp.bfloat16),
            pltpu.VMEM((RANK, COLS), jnp.bfloat16),
            pltpu.VMEM((COLS, ROWS), jnp.bfloat16),
            pltpu.SemaphoreType.DMA((len(CHUNKS),)),
            pltpu.SemaphoreType.DMA((2,)),
            pltpu.SemaphoreType.DMA((len(CHUNKS),)),
        ],
        compiler_params=params(),
        cost_estimate=pl.CostEstimate(
            flops=2 * COLS * ROWS * RANK, bytes_accessed=8_500_000, transcendentals=0
        ),
        name="finish",
    )(right_sum, inverse, left, acc_a, acc_b)


def exchange(pieces, axes):
    return lax.all_to_all(pieces, axes, 0, 0, tiled=True)


def spread(total, count):
    return jnp.broadcast_to(total[None], (count,) + total.shape)


def sum_left(part, first, second):
    mine = jnp.sum(exchange(part.reshape(32, 16, LANES), PLANE), axis=0)
    mine, first = lax.optimization_barrier((mine, first))
    mine = jnp.sum(exchange(spread(mine, 8), Z), axis=0)
    total = exchange(spread(mine, 32), PLANE).reshape(part.shape)
    return total, (first, second)


def sum_right(part, work):
    mine = jnp.sum(exchange(part.reshape(8, 120, LANES), NEAR), axis=0)
    mine, work = lax.optimization_barrier((mine, work))
    mine = jnp.sum(exchange(spread(mine, 4), "zh"), axis=0)
    return exchange(spread(mine, 8), NEAR).reshape(part.shape), work


def local(activations, output_grads, error_buffer, right_start):
    grad, error = output_grads.T, error_buffer[0].T
    left_part = left_term(activations, grad, error, right_start.T)
    acc = [accumulate(half, activations, grad, error) for half in range(2)]
    left_sum, acc = sum_left(left_part, *acc)
    right_part = project(left_sum, *acc)
    right_sum, (inverse, left) = sum_right(right_part, orthonormal(left_sum))
    left_factor, right_factor, new_error = finish(right_sum, inverse, left, *acc)
    return (left_factor.T, right_factor.T, new_error.T[None])


def solution(mesh):
    fine = Mesh(mesh.devices.reshape(4, 4, 2, 4, 2), DP + ("y", "core"))
    tensor = ("y", "core")
    return jax.shard_map(
        local,
        mesh=fine,
        in_specs=(P(DP, None), P(DP, tensor), P(DP, None, tensor), P(tensor, None)),
        out_specs=(P(), P(tensor, None), P(DP, None, tensor)),
        check_vma=False,
    )
```
